32 devices in a mesh: row: 8 (over z, y), col: 4 (over x, core).
Axes of the slice: x: 2, y: 2, z: 4, core: 2. Of those that a mesh axis runs over, the one named last changes fastest.
Arguments:
- saved_input: bfloat16 [512, 49152], P('col', 'row'), may hold values from -6 to 6
- out_grad: bfloat16 [512, 12288], P('row', 'col'), may hold values from -0.75 to 0.75
- weight: bfloat16 [49152, 12288], P('row', 'col'), may hold values from -0.625 to 0.625
Outputs:
- in_grad: bfloat16 [512, 49152], P('col', 'row')
- weight_grad: bfloat16 [49152, 12288], P('row', 'col')
The draws below stay inside these ranges and needn't reach their ends.
All inputs are finite; a program needn't handle non-finite values.
Results may differ from the reference program's by a relative error of at most 0.0051.
Values may be sent and summed in bfloat16 or wider, within the bound.
A program may use at most 192 MiB of HBM per device.

```python
import math
import jax
import jax.numpy as jnp
from jax import lax

D = 12288
H = 49152
TOKENS = 512


def raised(array, key, source, target, parts, factor):
    owner, partner = [(jnp.arange(array.shape[axis_at]) // (array.shape[axis_at] // parts)).reshape([-1 if axis == axis_at else 1 for axis in range(array.ndim)]) for axis_at in (source, target)]
    chosen = jax.random.permutation(key, parts)[partner]
    strong = (owner == chosen) | (owner == (partner + parts // 2) % parts)
    return jnp.where(strong, factor * array, array)


def block_levels(rng, extent, shards, least, top_value):
    factor_of = 1.0
    for axis_at, blocks in shards:
        draws = jax.random.uniform(jax.random.fold_in(jax.random.fold_in(rng, 6), axis_at), (blocks,), jnp.float32, least / len(shards), top_value / len(shards))
        factor_of = factor_of * jnp.repeat(jnp.exp(draws), extent[axis_at] // blocks).reshape((-1,) + (1,) * (len(extent) - 1 - axis_at))
    return factor_of


def noise(key, shape, scale, reach, shards=(), held_as=jnp.bfloat16):
    result = scale * jax.random.normal(key, shape, jnp.float32)
    if shards:
        result = result * block_levels(key, shape, shards, -0.22, 0.18)
    return jnp.clip(result, -reach, reach).astype(held_as)


def gaussian_with(stream_key, shape, width, limit, cuts, heavy, kind=jnp.bfloat16):
    drawn = width * jax.random.normal(stream_key, shape, jnp.float32)
    if cuts:
        drawn = drawn * block_levels(stream_key, shape, cuts, -0.22, 0.18)
    return jnp.clip(raised(drawn, jax.random.fold_in(stream_key, 3), *heavy), -limit, limit).astype(kind)


def setup_inputs(seed: int = 0) -> dict:
    keys = jax.random.split(jax.random.key(seed), 4)
    return {
        "saved_input": noise(keys[0], (TOKENS, H), 1.0, 6.0, ((0, 4), (1, 8))),
        "out_grad": gaussian_with(keys[1], (TOKENS, D), (TOKENS // 4) ** -0.5, 0.75, ((0, 8), (1, 4)), (1, 0, 8, 2.0)),
        "weight": noise(keys[2], (H, D), (D // 128) ** -0.5, 0.625, ((0, 8), (1, 4))),
    }


def gelu_parts(values):
    coeff = math.sqrt(2.0 / math.pi)
    inner = jnp.tanh(coeff * (values + 0.044715 * values * values * values))
    gelu_value = 0.5 * values * (1.0 + inner)
    gelu_slope = 0.5 * (1.0 + inner) + 0.5 * values * (1.0 - inner * inner) * coeff * (1.0 + 3.0 * 0.044715 * values * values)
    return (gelu_value, gelu_slope)

def reference(saved_input, out_grad, weight):
    values = saved_input.astype(jnp.float32)
    gelu_value, gelu_slope = gelu_parts(values)
    hidden = gelu_value.astype(jnp.bfloat16)
    back = lax.dot_general(out_grad, weight, (((1,), (1,)), ((), ())), preferred_element_type=jnp.float32)
    in_grad = (back * gelu_slope).astype(jnp.bfloat16)
    weight_grad = lax.dot_general(hidden, out_grad, (((0,), (0,)), ((), ())), preferred_element_type=jnp.float32)
    return (in_grad, weight_grad.astype(jnp.bfloat16))
```

```python
import functools
import math

import jax
import jax.numpy as jnp
from jax import lax
from jax.experimental import pallas as pl
from jax.experimental.pallas import tpu as pltpu
from jax.sharding import PartitionSpec as P

MESH = pl.DeviceIdType.MESH
GRAD_CHUNKS = 2
HIDDEN_CHUNKS = 4
BACK_CHUNKS = 4


def gelu_parts(values):
    coeff = math.sqrt(2.0 / math.pi)
    square = values * values
    inner = jnp.tanh(coeff * (values + 0.044715 * square * values))
    half = 0.5 * (1.0 + inner)
    gelu_slope = half + 0.5 * values * (1.0 - inner * inner) * (
        coeff + (coeff * 3.0 * 0.044715) * square
    )
    return (values * half, gelu_slope)


def gather_kernel(
    sizes,
    saved,
    grad,
    grad_all,
    hidden_all,
    slope,
    hidden,
    local_sem,
    up_send,
    up_recv,
    down_send,
    down_recv,
    y_send,
    y_recv,
    x_send,
    x_recv,
    core_send,
    core_recv,
):
    n_z, n_y, n_x = sizes
    row, col = lax.axis_index("row"), lax.axis_index("col")
    z, y = row // n_y, row % n_y
    x, core = col // 2, col % 2
    twin = (row, x * 2 + (1 - core))
    above = (row + n_y, col)
    below = (row - n_y, col)
    y_peer = [None] + [(z * n_y + (y + k) % n_y, col) for k in range(1, n_y)]
    x_peer = [None] + [(row, ((x + k) % n_x) * 2 + core) for k in range(1, n_x)]
    x_from = [x] + [(x + n_x - k) % n_x for k in range(1, n_x)]
    has_above, has_below = z < n_z - 1, z > 0

    barrier = pltpu.get_barrier_semaphore()

    def greet(device):
        pl.semaphore_signal(barrier, inc=1, device_id=device, device_id_type=MESH)

    for device in [twin] + y_peer[1:] + x_peer[1:]:
        greet(device)

    @pl.when(has_above)
    def _():
        greet(above)

    @pl.when(has_below)
    def _():
        greet(below)

    ends = jnp.where(has_above, 1, 0) + jnp.where(has_below, 1, 0)
    pl.semaphore_wait(barrier, n_y + n_x - 1 + ends)

    tokens, width = grad.shape
    part = tokens // GRAD_CHUNKS
    own_tokens, units = saved.shape
    piece = own_tokens // HIDDEN_CHUNKS

    def grad_rows(source_z, c):
        start = (source_z * n_y + y) * tokens + c * part
        return grad_all.at[pl.ds(pl.multiple_of(start, 16), part)]

    def own_grad(c):
        return grad.at[pl.ds(c * part, part)]

    def hidden_rows(source_x, q):
        start = (source_x * 2 + core) * own_tokens + q * piece
        return hidden_all.at[pl.ds(pl.multiple_of(start, 16), piece)]

    def remote(source, target, send, recv, device):
        return pltpu.make_async_remote_copy(
            src_ref=source, dst_ref=target, send_sem=send, recv_sem=recv,
            device_id=device, device_id_type=MESH,
        )

    def up(i, c):
        block = grad_rows(z - i, c)
        at = i * GRAD_CHUNKS + c
        return remote(own_grad(c) if i == 0 else block, block, up_send.at[at], up_recv.at[at], above)

    def down(i, c):
        block = grad_rows(z + i, c)
        at = i * GRAD_CHUNKS + c
        return remote(own_grad(c) if i == 0 else block, block, down_send.at[at], down_recv.at[at], below)

    def across(slot, k, c):
        if slot == 0:
            block = grad_rows(z, c)
            source = own_grad(c)
        elif slot < n_z:
            block = source = grad_rows(z - slot, c)
        else:
            block = source = grad_rows(z + (slot - n_z + 1), c)
        at = (slot * (n_y - 1) + k - 1) * GRAD_CHUNKS + c
        return remote(source, block, y_send.at[at], y_recv.at[at], y_peer[k])

    def along(k, q):
        at = (k - 1) * HIDDEN_CHUNKS + q
        return remote(
            hidden.at[pl.ds(q * piece, piece)], hidden_rows(x, q), x_send.at[at], x_recv.at[at], x_peer[k]
        )

    def to_twin(k, q):
        block = hidden_rows(x_from[k], q)
        at = k * HIDDEN_CHUNKS + q
        source = hidden.at[pl.ds(q * piece, piece)] if k == 0 else block
        return remote(source, block, core_send.at[at], core_recv.at[at], twin)

    def keep(q):
        return pltpu.make_async_copy(
            hidden.at[pl.ds(q * piece, piece)], hidden_rows(x, q), local_sem.at[GRAD_CHUNKS + q]
        )

    def keep_grad(c):
        return pltpu.make_async_copy(own_grad(c), grad_rows(z, c), local_sem.at[c])

    def can_send_up(i):
        return jnp.logical_and(has_above, z >= i)

    def can_send_down(i):
        return jnp.logical_and(has_below, z + i < n_z)

    for c in range(GRAD_CHUNKS):

        @pl.when(has_above)
        def _():
            up(0, c).start()

        @pl.when(has_below)
        def _():
            down(0, c).start()

        for k in range(1, n_y):
            across(0, k, c).start()

    tile = 512 if units % 512 == 0 else 128
    for q in range(HIDDEN_CHUNKS):
        rows = pl.ds(q * piece, piece)

        def body(j, carry):
            columns = pl.ds(pl.multiple_of(j * tile, tile), tile)
            value, gelu_slope = gelu_parts(saved[rows, columns].astype(jnp.float32))
            hidden[rows, columns] = value.astype(jnp.bfloat16)
            slope[rows, columns] = gelu_slope
            return carry

        lax.fori_loop(0, units // tile, body, 0)
        for k in range(1, n_x):
            along(k, q).start()
        to_twin(0, q).start()
        keep(q).start()

    for c in range(GRAD_CHUNKS):
        keep_grad(c).start()

    hidden_arrivals = [(k, q) for q in range(HIDDEN_CHUNKS) for k in range(1, n_x)]

    def forward_hidden(k, q):
        along(k, q).wait_recv()
        to_twin(k, q).start()

    done = 0
    for i in range(n_z - 1):
        for c in range(GRAD_CHUNKS):

            @pl.when(z > i)
            def _():
                up(i, c).wait_recv()

                @pl.when(has_above)
                def _():
                    if i + 1 < n_z - 1:
                        up(i + 1, c).start()

                for k in range(1, n_y):
                    across(1 + i, k, c).start()

            @pl.when(z + 1 + i < n_z)
            def _():
                down(i, c).wait_recv()

                @pl.when(has_below)
                def _():
                    if i + 1 < n_z - 1:
                        down(i + 1, c).start()

                for k in range(1, n_y):
                    across(n_z + i, k, c).start()

        upto = (i + 1) * len(hidden_arrivals) // n_z
        for k, q in hidden_arrivals[done:upto]:
            forward_hidden(k, q)
        done = upto
    for k, q in hidden_arrivals[done:]:
        forward_hidden(k, q)

    for c in range(GRAD_CHUNKS):
        keep_grad(c).wait()
        for i in range(n_z - 1):

            @pl.when(can_send_up(i))
            def _():
                up(i, c).wait_send()

            @pl.when(can_send_down(i))
            def _():
                down(i, c).wait_send()

        for k in range(1, n_y):
            across(0, k, c).wait()
            for i in range(n_z - 1):

                @pl.when(z > i)
                def _():
                    across(1 + i, k, c).wait()

                @pl.when(z + 1 + i < n_z)
                def _():
                    across(n_z + i, k, c).wait()

    for q in range(HIDDEN_CHUNKS):
        keep(q).wait()
        for k in range(1, n_x):
            along(k, q).wait_send()
        for k in range(n_x):
            to_twin(k, q).wait()


def gather(sizes, saved_input, out_grad):
    n_z, n_y, n_x = sizes
    own_tokens, units = saved_input.shape
    tokens, width = out_grad.shape
    dma = pltpu.SemaphoreType.DMA
    line = (n_z - 1) * GRAD_CHUNKS
    across = (2 * n_z - 1) * (n_y - 1) * GRAD_CHUNKS
    return pl.pallas_call(
        functools.partial(gather_kernel, sizes),
        out_shape=(
            jax.ShapeDtypeStruct((n_z * n_y * tokens, width), jnp.bfloat16),
            jax.ShapeDtypeStruct((2 * n_x * own_tokens, units), jnp.bfloat16),
            jax.ShapeDtypeStruct((own_tokens, units), jnp.float32),
        ),
        in_specs=[
            pl.BlockSpec(memory_space=pltpu.VMEM),
            pl.BlockSpec(memory_space=pl.ANY),
        ],
        out_specs=(
            pl.BlockSpec(memory_space=pl.ANY),
            pl.BlockSpec(memory_space=pl.ANY),
            pl.BlockSpec(memory_space=pltpu.VMEM),
        ),
        scratch_shapes=[
            pltpu.VMEM((own_tokens, units), jnp.bfloat16),
            dma((GRAD_CHUNKS + HIDDEN_CHUNKS,)),
            dma((line,)),
            dma((line,)),
            dma((line,)),
            dma((line,)),
            dma((across,)),
            dma((across,)),
            dma(((n_x - 1) * HIDDEN_CHUNKS,)),
            dma(((n_x - 1) * HIDDEN_CHUNKS,)),
            dma((n_x * HIDDEN_CHUNKS,)),
            dma((n_x * HIDDEN_CHUNKS,)),
        ],
        compiler_params=pltpu.CompilerParams(
            collective_id=0, has_side_effects=True, vmem_limit_bytes=32 * 1024 * 1024
        ),
    )(saved_input, out_grad)


def per_device(sizes, saved_input, out_grad, weight):
    n_z, n_y, n_x = sizes
    grad_all, hidden_all, slope = gather(sizes, saved_input, out_grad)
    col = lax.axis_index("col")
    x, core = col // 2, col % 2
    own_tokens, units = saved_input.shape
    pair = 2 * own_tokens
    swap_core = [(d, d ^ 1) for d in range(2 * n_x)]
    chunk = units // BACK_CHUNKS

    def pair_sum(owner_x, weights):
        grads = lax.dynamic_slice_in_dim(grad_all, owner_x * pair, pair, 0)
        product = lax.dot_general(
            grads, weights, (((1,), (1,)), ((), ())), preferred_element_type=jnp.float32
        )
        mine = lax.dynamic_slice_in_dim(product, core * own_tokens, own_tokens, 0)
        theirs = lax.dynamic_slice_in_dim(product, (1 - core) * own_tokens, own_tokens, 0)
        got = lax.ppermute(theirs.astype(jnp.bfloat16), "col", swap_core)
        return mine + got.astype(jnp.float32)

    sent = {}
    for j in range(BACK_CHUNKS):
        weights = weight[j * chunk : (j + 1) * chunk]
        for k in range(1, n_x):
            shift = [(d, (d + 2 * k) % (2 * n_x)) for d in range(2 * n_x)]
            total = pair_sum((x + k) % n_x, weights).astype(jnp.bfloat16)
            sent[j, k] = lax.ppermute(total, "col", shift)
    back = pair_sum(x, weight)
    weight_grad = lax.dot_general(
        hidden_all, grad_all, (((0,), (0,)), ((), ())), preferred_element_type=jnp.float32
    ).astype(jnp.bfloat16)
    for k in range(1, n_x):
        back = back + jnp.concatenate(
            [sent[j, k] for j in range(BACK_CHUNKS)], axis=1
        ).astype(jnp.float32)
    in_grad = (back * slope).astype(jnp.bfloat16)
    return (in_grad, weight_grad)


def solution(mesh):
    n_x = mesh.shape["col"] // 2
    n_y = n_x if mesh.shape["row"] % n_x == 0 else 1
    sizes = (mesh.shape["row"] // n_y, n_y, n_x)
    in_specs = (P("col", "row"), P("row", "col"), P("row", "col"))
    out_specs = (P("col", "row"), P("row", "col"))
    return jax.shard_map(
        functools.partial(per_device, sizes),
        mesh=mesh,
        in_specs=in_specs,
        out_specs=out_specs,
        check_vma=False,
    )
```

```python
import functools
import math

import jax
import jax.numpy as jnp
from jax import lax
from jax.experimental import pallas as pl
from jax.experimental.pallas import tpu as pltpu
from jax.sharding import PartitionSpec as P

MESH = pl.DeviceIdType.MESH
GRAD_CHUNKS = 2
HIDDEN_CHUNKS = 8
BACK_CHUNKS = 3


def gelu_parts(values):
    coeff = math.sqrt(2.0 / math.pi)
    square = values * values
    inner = jnp.tanh(coeff * (values + 0.044715 * square * values))
    half = 0.5 * (1.0 + inner)
    gelu_slope = half + 0.5 * values * (1.0 - inner * inner) * (
        coeff + (coeff * 3.0 * 0.044715) * square
    )
    return (values * half, gelu_slope)


def gather_kernel(
    sizes,
    saved,
    grad,
    grad_all,
    hidden_all,
    slope,
    hidden,
    local_sem,
    up_send,
    up_recv,
    down_send,
    down_recv,
    y_send,
    y_recv,
    x_send,
    x_recv,
    core_send,
    core_recv,
):
    n_z, n_y, n_x = sizes
    row, col = lax.axis_index("row"), lax.axis_index("col")
    z, y = row // n_y, row % n_y
    x, core = col // 2, col % 2
    twin = (row, x * 2 + (1 - core))
    above = (row + n_y, col)
    below = (row - n_y, col)
    y_peer = [None] + [(z * n_y + (y + k) % n_y, col) for k in range(1, n_y)]
    x_peer = [None] + [(row, ((x + k) % n_x) * 2 + core) for k in range(1, n_x)]
    x_from = [x] + [(x + n_x - k) % n_x for k in range(1, n_x)]
    has_above, has_below = z < n_z - 1, z > 0

    barrier = pltpu.get_barrier_semaphore()

    def greet(device):
        pl.semaphore_signal(barrier, inc=1, device_id=device, device_id_type=MESH)

    for device in [twin] + y_peer[1:] + x_peer[1:]:
        greet(device)

    @pl.when(has_above)
    def _():
        greet(above)

    @pl.when(has_below)
    def _():
        greet(below)

    ends = jnp.where(has_above, 1, 0) + jnp.where(has_below, 1, 0)
    pl.semaphore_wait(barrier, n_y + n_x - 1 + ends)

    tokens, width = grad.shape
    part = tokens // GRAD_CHUNKS
    own_tokens, units = saved.shape
    piece = own_tokens // HIDDEN_CHUNKS

    def grad_rows(source_z, c):
        start = (source_z * n_y + y) * tokens + c * part
        return grad_all.at[pl.ds(pl.multiple_of(start, 16), part)]

    def own_grad(c):
        return grad.at[pl.ds(c * part, part)]

    def hidden_rows(source_x, q):
        start = (source_x * 2 + core) * own_tokens + q * piece
        return hidden_all.at[pl.ds(pl.multiple_of(start, 16), piece)]

    def remote(source, target, send, recv, device):
        return pltpu.make_async_remote_copy(
            src_ref=source, dst_ref=target, send_sem=send, recv_sem=recv,
            device_id=device, device_id_type=MESH,
        )

    def up(i, c):
        block = grad_rows(z - i, c)
        at = i * GRAD_CHUNKS + c
        return remote(own_grad(c) if i == 0 else block, block, up_send.at[at], up_recv.at[at], above)

    def down(i, c):
        block = grad_rows(z + i, c)
        at = i * GRAD_CHUNKS + c
        return remote(own_grad(c) if i == 0 else block, block, down_send.at[at], down_recv.at[at], below)

    def across(slot, k, c):
        if slot == 0:
            block = grad_rows(z, c)
            source = own_grad(c)
        elif slot < n_z:
            block = source = grad_rows(z - slot, c)
        else:
            block = source = grad_rows(z + (slot - n_z + 1), c)
        at = (slot * (n_y - 1) + k - 1) * GRAD_CHUNKS + c
        return remote(source, block, y_send.at[at], y_recv.at[at], y_peer[k])

    def along(k, q):
        at = (k - 1) * HIDDEN_CHUNKS + q
        return remote(
            hidden.at[pl.ds(q * piece, piece)], hidden_rows(x, q), x_send.at[at], x_recv.at[at], x_peer[k]
        )

    def to_twin(k, q):
        block = hidden_rows(x_from[k], q)
        at = k * HIDDEN_CHUNKS + q
        source = hidden.at[pl.ds(q * piece, piece)] if k == 0 else block
        return remote(source, block, core_send.at[at], core_recv.at[at], twin)

    def keep(q):
        return pltpu.make_async_copy(
            hidden.at[pl.ds(q * piece, piece)], hidden_rows(x, q), local_sem.at[GRAD_CHUNKS + q]
        )

    def keep_grad(c):
        return pltpu.make_async_copy(own_grad(c), grad_rows(z, c), local_sem.at[c])

    def can_send_up(i):
        return jnp.logical_and(has_above, z >= i)

    def can_send_down(i):
        return jnp.logical_and(has_below, z + i < n_z)

    for c in range(GRAD_CHUNKS):

        @pl.when(has_above)
        def _():
            up(0, c).start()

        @pl.when(has_below)
        def _():
            down(0, c).start()

        for k in range(1, n_y):
            across(0, k, c).start()

    tile = 512 if units % 512 == 0 else 128
    for q in range(HIDDEN_CHUNKS):
        rows = pl.ds(q * piece, piece)

        def body(j, carry):
            columns = pl.ds(pl.multiple_of(j * tile, tile), tile)
            value, unused_slope = gelu_parts(saved[rows, columns].astype(jnp.float32))
            hidden[rows, columns] = value.astype(jnp.bfloat16)
            return carry

        lax.fori_loop(0, units // tile, body, 0)
        for k in range(1, n_x):
            along(k, q).start()
        to_twin(0, q).start()
        keep(q).start()

    for c in range(GRAD_CHUNKS):
        keep_grad(c).start()

    for q in range(HIDDEN_CHUNKS):
        rows = pl.ds(q * piece, piece)

        def slope_body(j, carry):
            columns = pl.ds(pl.multiple_of(j * tile, tile), tile)
            unused_value, gelu_slope = gelu_parts(saved[rows, columns].astype(jnp.float32))
            slope[rows, columns] = gelu_slope
            return carry

        lax.fori_loop(0, units // tile, slope_body, 0)

    hidden_arrivals = [(k, q) for q in range(HIDDEN_CHUNKS) for k in range(1, n_x)]

    def forward_hidden(k, q):
        along(k, q).wait_recv()
        to_twin(k, q).start()

    done = 0
    for i in range(n_z - 1):
        for c in range(GRAD_CHUNKS):

            @pl.when(z > i)
            def _():
                up(i, c).wait_recv()

                @pl.when(has_above)
                def _():
                    if i + 1 < n_z - 1:
                        up(i + 1, c).start()

                for k in range(1, n_y):
                    across(1 + i, k, c).start()

            @pl.when(z + 1 + i < n_z)
            def _():
                down(i, c).wait_recv()

                @pl.when(has_below)
                def _():
                    if i + 1 < n_z - 1:
                        down(i + 1, c).start()

                for k in range(1, n_y):
                    across(n_z + i, k, c).start()

        upto = (i + 1) * len(hidden_arrivals) // n_z
        for k, q in hidden_arrivals[done:upto]:
            forward_hidden(k, q)
        done = upto
    for k, q in hidden_arrivals[done:]:
        forward_hidden(k, q)

    for c in range(GRAD_CHUNKS):
        keep_grad(c).wait()
        for i in range(n_z - 1):

            @pl.when(can_send_up(i))
            def _():
                up(i, c).wait_send()

            @pl.when(can_send_down(i))
            def _():
                down(i, c).wait_send()

        for k in range(1, n_y):
            across(0, k, c).wait()
            for i in range(n_z - 1):

                @pl.when(z > i)
                def _():
                    across(1 + i, k, c).wait()

                @pl.when(z + 1 + i < n_z)
                def _():
                    across(n_z + i, k, c).wait()

    for q in range(HIDDEN_CHUNKS):
        keep(q).wait()
        for k in range(1, n_x):
            along(k, q).wait_send()
        for k in range(n_x):
            to_twin(k, q).wait()


def gather(sizes, saved_input, out_grad):
    n_z, n_y, n_x = sizes
    own_tokens, units = saved_input.shape
    tokens, width = out_grad.shape
    dma = pltpu.SemaphoreType.DMA
    line = (n_z - 1) * GRAD_CHUNKS
    across = (2 * n_z - 1) * (n_y - 1) * GRAD_CHUNKS
    return pl.pallas_call(
        functools.partial(gather_kernel, sizes),
        out_shape=(
            jax.ShapeDtypeStruct((n_z * n_y * tokens, width), jnp.bfloat16),
            jax.ShapeDtypeStruct((2 * n_x * own_tokens, units), jnp.bfloat16),
            jax.ShapeDtypeStruct((own_tokens, units), jnp.float32),
        ),
        in_specs=[
            pl.BlockSpec(memory_space=pltpu.VMEM),
            pl.BlockSpec(memory_space=pl.ANY),
        ],
        out_specs=(
            pl.BlockSpec(memory_space=pl.ANY),
            pl.BlockSpec(memory_space=pl.ANY),
            pl.BlockSpec(memory_space=pltpu.VMEM),
        ),
        scratch_shapes=[
            pltpu.VMEM((own_tokens, units), jnp.bfloat16),
            dma((GRAD_CHUNKS + HIDDEN_CHUNKS,)),
            dma((line,)),
            dma((line,)),
            dma((line,)),
            dma((line,)),
            dma((across,)),
            dma((across,)),
            dma(((n_x - 1) * HIDDEN_CHUNKS,)),
            dma(((n_x - 1) * HIDDEN_CHUNKS,)),
            dma((n_x * HIDDEN_CHUNKS,)),
            dma((n_x * HIDDEN_CHUNKS,)),
        ],
        compiler_params=pltpu.CompilerParams(
            collective_id=0, has_side_effects=True, vmem_limit_bytes=32 * 1024 * 1024
        ),
    )(saved_input, out_grad)


def back_kernel(n_x, place, grads, weights, mine, theirs, product):
    x, core = place[0], place[1]
    tokens = mine.shape[1]
    product[...] = lax.dot_general(
        grads[...], weights[...], (((1,), (1,)), ((), ())), preferred_element_type=jnp.float32
    )
    for k in range(n_x):
        owner = lax.rem(x + k, n_x) * 2
        own_start = pl.multiple_of((owner + core) * tokens, tokens)
        twin_start = pl.multiple_of((owner + 1 - core) * tokens, tokens)
        mine[k] = product[pl.ds(own_start, tokens), :].astype(jnp.bfloat16)
        theirs[k] = product[pl.ds(twin_start, tokens), :].astype(jnp.bfloat16)


def back_part(n_x, own_tokens, place, grad_all, weight, j):
    tokens, width = grad_all.shape
    chunk = weight.shape[0] // BACK_CHUNKS
    tile = 256 if chunk % 256 == 0 else 128
    steps = chunk // tile
    result = jax.ShapeDtypeStruct((n_x, own_tokens, chunk), jnp.bfloat16)
    block = pl.BlockSpec((n_x, own_tokens, tile), lambda i, place: (0, 0, i))
    return pl.pallas_call(
        functools.partial(back_kernel, n_x),
        out_shape=(result, result),
        grid_spec=pltpu.PrefetchScalarGridSpec(
            num_scalar_prefetch=1,
            grid=(steps,),
            in_specs=[
                pl.BlockSpec((tokens, width), lambda i, place: (0, 0)),
                pl.BlockSpec((tile, width), lambda i, place: (j * steps + i, 0)),
            ],
            out_specs=(block, block),
            scratch_shapes=[pltpu.VMEM((tokens, tile), jnp.float32)],
        ),
        compiler_params=pltpu.CompilerParams(vmem_limit_bytes=32 * 1024 * 1024),
        cost_estimate=pl.CostEstimate(
            flops=2 * tokens * width * chunk, bytes_accessed=2 * chunk * width, transcendentals=0
        ),
    )(place, grad_all, weight)


def weight_grad_kernel(tile, hidden, grads, result):
    turned = hidden[...].T
    width = result.shape[1]

    def body(j, carry):
        columns = pl.ds(pl.multiple_of(j * tile, tile), tile)
        result[:, columns] = jnp.dot(
            turned, grads[:, columns], preferred_element_type=jnp.float32
        ).astype(jnp.bfloat16)
        return carry

    lax.fori_loop(0, width // tile, body, 0)


def weight_grad_of(hidden_all, grad_all):
    tokens, units = hidden_all.shape
    width = grad_all.shape[1]
    rows = 512 if units % 512 == 0 else 128
    tile = 512 if width % 512 == 0 else 128
    return pl.pallas_call(
        functools.partial(weight_grad_kernel, tile),
        out_shape=jax.ShapeDtypeStruct((units, width), jnp.bfloat16),
        grid=(units // rows,),
        in_specs=[
            pl.BlockSpec((tokens, rows), lambda i: (0, i)),
            pl.BlockSpec((tokens, width), lambda i: (0, 0)),
        ],
        out_specs=pl.BlockSpec((rows, width), lambda i: (i, 0)),
        compiler_params=pltpu.CompilerParams(vmem_limit_bytes=32 * 1024 * 1024),
        cost_estimate=pl.CostEstimate(
            flops=2 * tokens * units * width, bytes_accessed=2 * units * width, transcendentals=0
        ),
    )(hidden_all, grad_all)


def finish_kernel(n_terms, *refs):
    slope, result = refs[-2], refs[-1]
    for j in range(BACK_CHUNKS):
        terms = refs[j * n_terms : (j + 1) * n_terms]
        chunk = terms[0].shape[2]
        for start in range(0, chunk, 128):
            columns = slice(start, start + 128)
            back = terms[0][0, :, columns].astype(jnp.float32) + terms[1][0, :, columns].astype(jnp.float32)
            for term in terms[2:]:
                back = back + term[:, columns].astype(jnp.float32)
            target = slice(j * chunk + start, j * chunk + start + 128)
            result[:, target] = (back * slope[:, target]).astype(jnp.bfloat16)


def per_device(sizes, saved_input, out_grad, weight):
    n_z, n_y, n_x = sizes
    grad_all, hidden_all, slope = gather(sizes, saved_input, out_grad)
    col = lax.axis_index("col")
    x, core = col // 2, col % 2
    place = jnp.stack([x, core]).astype(jnp.int32)
    own_tokens = saved_input.shape[0]
    swap_core = [(d, d ^ 1) for d in range(2 * n_x)]

    terms = []
    for j in range(BACK_CHUNKS):
        mine, theirs = back_part(n_x, own_tokens, place, grad_all, weight, j)
        got = lax.ppermute(theirs, "col", swap_core)
        terms += [mine, got]
        for k in range(1, n_x):
            shift = [(d, (d + 2 * k) % (2 * n_x)) for d in range(2 * n_x)]
            total = mine[k].astype(jnp.float32) + got[k].astype(jnp.float32)
            terms.append(lax.ppermute(total.astype(jnp.bfloat16), "col", shift))
    weight_grad = weight_grad_of(hidden_all, grad_all)
    in_grad = pl.pallas_call(
        functools.partial(finish_kernel, n_x + 1),
        out_shape=jax.ShapeDtypeStruct(saved_input.shape, jnp.bfloat16),
        in_specs=[pl.BlockSpec(memory_space=pltpu.VMEM)] * (len(terms) + 1),
        out_specs=pl.BlockSpec(memory_space=pltpu.VMEM),
        compiler_params=pltpu.CompilerParams(vmem_limit_bytes=32 * 1024 * 1024),
    )(*terms, slope)
    return (in_grad, weight_grad)


def solution(mesh):
    n_x = mesh.shape["col"] // 2
    n_y = n_x if mesh.shape["row"] % n_x == 0 else 1
    sizes = (mesh.shape["row"] // n_y, n_y, n_x)
    in_specs = (P("col", "row"), P("row", "col"), P("row", "col"))
    out_specs = (P("col", "row"), P("row", "col"))
    return jax.shard_map(
        functools.partial(per_device, sizes),
        mesh=mesh,
        in_specs=in_specs,
        out_specs=out_specs,
        check_vma=False,
    )
```

```python
import functools
import math

import jax
import jax.numpy as jnp
from jax import lax
from jax.experimental import pallas as pl
from jax.experimental.pallas import tpu as pltpu
from jax.sharding import PartitionSpec as P

MESH = pl.DeviceIdType.MESH
GRAD_CHUNKS = 2
HIDDEN_CHUNKS = 8
BACK_CHUNKS = 3


def gelu_parts(values):
    coeff = math.sqrt(2.0 / math.pi)
    square = values * values
    inner = jnp.tanh(coeff * (values + 0.044715 * square * values))
    half = 0.5 * (1.0 + inner)
    gelu_slope = half + 0.5 * values * (1.0 - inner * inner) * (
        coeff + (coeff * 3.0 * 0.044715) * square
    )
    return (values * half, gelu_slope)


def gather_kernel(
    sizes,
    saved,
    grad,
    grad_all,
    hidden_all,
    slope,
    hidden,
    local_sem,
    up_send,
    up_recv,
    down_send,
    down_recv,
    y_send,
    y_recv,
    x_send,
    x_recv,
    core_send,
    core_recv,
):
    n_z, n_y, n_x = sizes
    row, col = lax.axis_index("row"), lax.axis_index("col")
    z, y = row // n_y, row % n_y
    x, core = col // 2, col % 2
    twin = (row, x * 2 + (1 - core))
    above = (row + n_y, col)
    below = (row - n_y, col)
    y_peer = [None] + [(z * n_y + (y + k) % n_y, col) for k in range(1, n_y)]
    x_peer = [None] + [(row, ((x + k) % n_x) * 2 + core) for k in range(1, n_x)]
    x_from = [x] + [(x + n_x - k) % n_x for k in range(1, n_x)]
    has_above, has_below = z < n_z - 1, z > 0

    barrier = pltpu.get_barrier_semaphore()

    def greet(device):
        pl.semaphore_signal(barrier, inc=1, device_id=device, device_id_type=MESH)

    for device in [twin] + y_peer[1:] + x_peer[1:]:
        greet(device)

    @pl.when(has_above)
    def _():
        greet(above)

    @pl.when(has_below)
    def _():
        greet(below)

    ends = jnp.where(has_above, 1, 0) + jnp.where(has_below, 1, 0)
    pl.semaphore_wait(barrier, n_y + n_x - 1 + ends)

    tokens, width = grad.shape
    part = tokens // GRAD_CHUNKS
    own_tokens, units = saved.shape
    piece = own_tokens // HIDDEN_CHUNKS

    def grad_rows(source_z, c):
        start = (source_z * n_y + y) * tokens + c * part
        return grad_all.at[pl.ds(pl.multiple_of(start, 16), part)]

    def own_grad(c):
        return grad.at[pl.ds(c * part, part)]

    def hidden_rows(source_x, q):
        start = (source_x * 2 + core) * own_tokens + q * piece
        return hidden_all.at[pl.ds(pl.multiple_of(start, 16), piece)]

    def remote(source, target, send, recv, device):
        return pltpu.make_async_remote_copy(
            src_ref=source, dst_ref=target, send_sem=send, recv_sem=recv,
            device_id=device, device_id_type=MESH,
        )

    def up(i, c):
        block = grad_rows(z - i, c)
        at = i * GRAD_CHUNKS + c
        return remote(own_grad(c) if i == 0 else block, block, up_send.at[at], up_recv.at[at], above)

    def down(i, c):
        block = grad_rows(z + i, c)
        at = i * GRAD_CHUNKS + c
        return remote(own_grad(c) if i == 0 else block, block, down_send.at[at], down_recv.at[at], below)

    def across(slot, k, c):
        if slot == 0:
            block = grad_rows(z, c)
            source = own_grad(c)
        elif slot < n_z:
            block = source = grad_rows(z - slot, c)
        else:
            block = source = grad_rows(z + (slot - n_z + 1), c)
        at = (slot * (n_y - 1) + k - 1) * GRAD_CHUNKS + c
        return remote(source, block, y_send.at[at], y_recv.at[at], y_peer[k])

    def along(k, q):
        at = (k - 1) * HIDDEN_CHUNKS + q
        return remote(
            hidden.at[pl.ds(q * piece, piece)], hidden_rows(x, q), x_send.at[at], x_recv.at[at], x_peer[k]
        )

    def to_twin(k, q):
        block = hidden_rows(x_from[k], q)
        at = k * HIDDEN_CHUNKS + q
        source = hidden.at[pl.ds(q * piece, piece)] if k == 0 else block
        return remote(source, block, core_send.at[at], core_recv.at[at], twin)

    def keep(q):
        return pltpu.make_async_copy(
            hidden.at[pl.ds(q * piece, piece)], hidden_rows(x, q), local_sem.at[GRAD_CHUNKS + q]
        )

    def keep_grad(c):
        return pltpu.make_async_copy(own_grad(c), grad_rows(z, c), local_sem.at[c])

    def can_send_up(i):
        return jnp.logical_and(has_above, z >= i)

    def can_send_down(i):
        return jnp.logical_and(has_below, z + i < n_z)

    for c in range(GRAD_CHUNKS):

        @pl.when(has_above)
        def _():
            up(0, c).start()

        @pl.when(has_below)
        def _():
            down(0, c).start()

        for k in range(1, n_y):
            across(0, k, c).start()

    tile = 512 if units % 512 == 0 else 128
    for q in range(HIDDEN_CHUNKS):
        rows = pl.ds(q * piece, piece)

        def body(j, carry):
            columns = pl.ds(pl.multiple_of(j * tile, tile), tile)
            value, unused_slope = gelu_parts(saved[rows, columns].astype(jnp.float32))
            hidden[rows, columns] = value.astype(jnp.bfloat16)
            return carry

        lax.fori_loop(0, units // tile, body, 0)
        for k in range(1, n_x):
            along(k, q).start()
        to_twin(0, q).start()
        keep(q).start()

    for c in range(GRAD_CHUNKS):
        keep_grad(c).start()

    for q in range(HIDDEN_CHUNKS):
        rows = pl.ds(q * piece, piece)

        def slope_body(j, carry):
            columns = pl.ds(pl.multiple_of(j * tile, tile), tile)
            unused_value, gelu_slope = gelu_parts(saved[rows, columns].astype(jnp.float32))
            slope[rows, columns] = gelu_slope
            return carry

        lax.fori_loop(0, units // tile, slope_body, 0)

    hidden_arrivals = [(k, q) for q in range(HIDDEN_CHUNKS) for k in range(1, n_x)]

    def forward_hidden(k, q):
        along(k, q).wait_recv()
        to_twin(k, q).start()

    done = 0
    for i in range(n_z - 1):
        for c in range(GRAD_CHUNKS):

            @pl.when(z > i)
            def _():
                up(i, c).wait_recv()

                @pl.when(has_above)
                def _():
                    if i + 1 < n_z - 1:
                        up(i + 1, c).start()

                for k in range(1, n_y):
                    across(1 + i, k, c).start()

            @pl.when(z + 1 + i < n_z)
            def _():
                down(i, c).wait_recv()

                @pl.when(has_below)
                def _():
                    if i + 1 < n_z - 1:
                        down(i + 1, c).start()

                for k in range(1, n_y):
                    across(n_z + i, k, c).start()

        upto = (i + 1) * len(hidden_arrivals) // n_z
        for k, q in hidden_arrivals[done:upto]:
            forward_hidden(k, q)
        done = upto
    for k, q in hidden_arrivals[done:]:
        forward_hidden(k, q)

    for c in range(GRAD_CHUNKS):
        keep_grad(c).wait()
        for i in range(n_z - 1):

            @pl.when(can_send_up(i))
            def _():
                up(i, c).wait_send()

            @pl.when(can_send_down(i))
            def _():
                down(i, c).wait_send()

        for k in range(1, n_y):
            across(0, k, c).wait()
            for i in range(n_z - 1):

                @pl.when(z > i)
                def _():
                    across(1 + i, k, c).wait()

                @pl.when(z + 1 + i < n_z)
                def _():
                    across(n_z + i, k, c).wait()

    for q in range(HIDDEN_CHUNKS):
        keep(q).wait()
        for k in range(1, n_x):
            along(k, q).wait_send()
        for k in range(n_x):
            to_twin(k, q).wait()


def gather(sizes, saved_input, out_grad):
    n_z, n_y, n_x = sizes
    own_tokens, units = saved_input.shape
    tokens, width = out_grad.shape
    dma = pltpu.SemaphoreType.DMA
    line = (n_z - 1) * GRAD_CHUNKS
    across = (2 * n_z - 1) * (n_y - 1) * GRAD_CHUNKS
    return pl.pallas_call(
        functools.partial(gather_kernel, sizes),
        out_shape=(
            jax.ShapeDtypeStruct((n_z * n_y * tokens, width), jnp.bfloat16),
            jax.ShapeDtypeStruct((2 * n_x * own_tokens, units), jnp.bfloat16),
            jax.ShapeDtypeStruct((own_tokens, units), jnp.float32),
        ),
        in_specs=[
            pl.BlockSpec(memory_space=pltpu.VMEM),
            pl.BlockSpec(memory_space=pl.ANY),
        ],
        out_specs=(
            pl.BlockSpec(memory_space=pl.ANY),
            pl.BlockSpec(memory_space=pl.ANY),
            pl.BlockSpec(memory_space=pltpu.VMEM),
        ),
        scratch_shapes=[
            pltpu.VMEM((own_tokens, units), jnp.bfloat16),
            dma((GRAD_CHUNKS + HIDDEN_CHUNKS,)),
            dma((line,)),
            dma((line,)),
            dma((line,)),
            dma((line,)),
            dma((across,)),
            dma((across,)),
            dma(((n_x - 1) * HIDDEN_CHUNKS,)),
            dma(((n_x - 1) * HIDDEN_CHUNKS,)),
            dma((n_x * HIDDEN_CHUNKS,)),
            dma((n_x * HIDDEN_CHUNKS,)),
        ],
        compiler_params=pltpu.CompilerParams(
            collective_id=0, has_side_effects=True, vmem_limit_bytes=32 * 1024 * 1024
        ),
    )(saved_input, out_grad)


def back_kernel(n_x, place, grads, weights, mine, theirs, product):
    x, core = place[0], place[1]
    tokens = mine.shape[1]
    sums = jnp.dot(weights[...], grads[...], preferred_element_type=jnp.float32)
    product[...] = sums.astype(jnp.bfloat16).T
    for k in range(n_x):
        owner = lax.rem(x + k, n_x) * 2
        own_start = pl.multiple_of((owner + core) * tokens, tokens)
        twin_start = pl.multiple_of((owner + 1 - core) * tokens, tokens)
        mine[k] = product[pl.ds(own_start, tokens), :]
        theirs[k] = product[pl.ds(twin_start, tokens), :]


def back_part(n_x, own_tokens, place, turned, weight, j):
    width, tokens = turned.shape
    chunk = weight.shape[0] // BACK_CHUNKS
    tile = 512 if chunk % 512 == 0 else 128
    steps = chunk // tile
    result = jax.ShapeDtypeStruct((n_x, own_tokens, chunk), jnp.bfloat16)
    block = pl.BlockSpec((n_x, own_tokens, tile), lambda i, place: (0, 0, i))
    return pl.pallas_call(
        functools.partial(back_kernel, n_x),
        out_shape=(result, result),
        grid_spec=pltpu.PrefetchScalarGridSpec(
            num_scalar_prefetch=1,
            grid=(steps,),
            in_specs=[
                pl.BlockSpec((width, tokens), lambda i, place: (0, 0)),
                pl.BlockSpec((tile, width), lambda i, place: (j * steps + i, 0)),
            ],
            out_specs=(block, block),
            scratch_shapes=[pltpu.VMEM((tokens, tile), jnp.bfloat16)],
        ),
        compiler_params=pltpu.CompilerParams(vmem_limit_bytes=32 * 1024 * 1024),
        cost_estimate=pl.CostEstimate(
            flops=2 * tokens * width * chunk, bytes_accessed=2 * chunk * width, transcendentals=0
        ),
    )(place, turned, weight)


def finish_kernel(n_terms, *refs):
    slope, result = refs[-2], refs[-1]
    for j in range(BACK_CHUNKS):
        terms = refs[j * n_terms : (j + 1) * n_terms]
        chunk = terms[0].shape[2]
        for start in range(0, chunk, 128):
            columns = slice(start, start + 128)
            back = terms[0][0, :, columns].astype(jnp.float32) + terms[1][0, :, columns].astype(jnp.float32)
            for term in terms[2:]:
                back = back + term[:, columns].astype(jnp.float32)
            target = slice(j * chunk + start, j * chunk + start + 128)
            result[:, target] = (back * slope[:, target]).astype(jnp.bfloat16)


def per_device(sizes, saved_input, out_grad, weight):
    n_z, n_y, n_x = sizes
    grad_all, hidden_all, slope = gather(sizes, saved_input, out_grad)
    col = lax.axis_index("col")
    x, core = col // 2, col % 2
    place = jnp.stack([x, core]).astype(jnp.int32)
    own_tokens = saved_input.shape[0]
    swap_core = [(d, d ^ 1) for d in range(2 * n_x)]

    turned = grad_all.T
    terms, totals = [], []
    for j in range(BACK_CHUNKS):
        if j > 1:
            place, *totals[j - 2] = lax.optimization_barrier((place, *totals[j - 2]))
        mine, theirs = back_part(n_x, own_tokens, place, turned, weight, j)
        got = lax.ppermute(theirs, "col", swap_core)
        terms.append([mine, got])
        totals.append(
            [
                (mine[k].astype(jnp.float32) + got[k].astype(jnp.float32)).astype(jnp.bfloat16)
                for k in range(1, n_x)
            ]
        )
    for j in range(BACK_CHUNKS):
        for k in range(1, n_x):
            shift = [(d, (d + 2 * k) % (2 * n_x)) for d in range(2 * n_x)]
            terms[j].append(lax.ppermute(totals[j][k - 1], "col", shift))
    terms = sum(terms, [])
    weight_grad = lax.dot_general(
        hidden_all, grad_all, (((0,), (0,)), ((), ())), preferred_element_type=jnp.float32
    ).astype(jnp.bfloat16)
    in_grad = pl.pallas_call(
        functools.partial(finish_kernel, n_x + 1),
        out_shape=jax.ShapeDtypeStruct(saved_input.shape, jnp.bfloat16),
        in_specs=[pl.BlockSpec(memory_space=pltpu.VMEM)] * (len(terms) + 1),
        out_specs=pl.BlockSpec(memory_space=pltpu.VMEM),
        compiler_params=pltpu.CompilerParams(vmem_limit_bytes=32 * 1024 * 1024),
    )(*terms, slope)
    return (in_grad, weight_grad)


def solution(mesh):
    n_x = mesh.shape["col"] // 2
    n_y = n_x if mesh.shape["row"] % n_x == 0 else 1
    sizes = (mesh.shape["row"] // n_y, n_y, n_x)
    in_specs = (P("col", "row"), P("row", "col"), P("row", "col"))
    out_specs = (P("col", "row"), P("row", "col"))
    return jax.shard_map(
        functools.partial(per_device, sizes),
        mesh=mesh,
        in_specs=in_specs,
        out_specs=out_specs,
        check_vma=False,
    )
```
